32 devices in a mesh: seq: 4 (over z), tm: 8 (over y, x, core).
Axes of the slice: x: 2, y: 2, z: 4, core: 2. Of those that a mesh axis runs over, the one named last changes fastest.
Arguments:
- inputs: float32 [4, 2048, 64], P('seq', 'tm'), may hold values from -6 to 6
- guess: float32 [4, 2048, 64], P('seq', 'tm'), may hold values from -0.9 to 0.9
- cotangent: float32 [4, 2048, 64], P('seq', 'tm'), may hold values from -0.4 to 0.4
- w_input: float32 [64, 192], replicated, may hold values from -0.75 to 0.75
- w_hidden: float32 [64, 192], replicated, may hold values from -0.75 to 0.75
- bias: float32 [256], replicated, may hold values from -2 to 13, as said below
Outputs:
- new_states: float32 [4, 2048, 64], P('seq', 'tm')
- adjoint: float32 [4, 2048, 64], P('seq', 'tm')
- grad_input: float32 [64, 192], replicated
- grad_hidden: float32 [64, 192], replicated
- grad_bias: float32 [256], replicated
The draws below stay inside these ranges and needn't reach their ends.
Inputs may be any that keep to these rules, and one draw needn't show every extreme that they name: `bias`: gate biases as laid out in the meaning.
All inputs are finite; a program needn't handle non-finite values.
Results may differ from the reference program's by a relative error of at most 0.00075.
Values sent between devices are 32-bit elements; how exact they have to be, the bound alone decides.
A program may use at most 128 MiB of HBM per device.

```python
import math
import jax
import jax.numpy as jnp
from jax import lax

D = 64
H = 64
SEQS = 4
SEQLEN = 2048


def draw_bias(key, part):
    keys = jax.random.split(key, 6)
    reset_part = jnp.clip(0.5 * jax.random.normal(keys[0], (H,), jnp.float32), -2.0, 2.0)
    slow_share = 0.5
    slow = jax.random.bernoulli(keys[1], slow_share, (H,))
    leak = jnp.exp(jax.random.uniform(keys[2], (H,), jnp.float32, jnp.log(0.5), jnp.log(3.0)))
    slow_bias = jnp.log(2.0 * SEQLEN / leak)
    fast_bias = jax.random.uniform(keys[3], (H,), jnp.float32, 1.0, 3.9)
    update_part = jnp.where(slow, slow_bias, fast_bias)
    cand_part = jnp.clip(0.5 * jax.random.normal(keys[4], (H,), jnp.float32), -2.0, 2.0)
    hidden_part = jnp.clip(0.5 * jax.random.normal(keys[5], (H,), jnp.float32), -2.0, 2.0)
    return jnp.concatenate([reset_part, update_part, cand_part, hidden_part]).astype(jnp.float32)


def levels(key, dims, cuts, smallest, top_value):
    level = 1.0
    for dim, blocks in cuts:
        draws = jax.random.uniform(jax.random.fold_in(jax.random.fold_in(key, 6), dim), (blocks,), jnp.float32, smallest / len(cuts), top_value / len(cuts))
        level = level * jnp.repeat(jnp.exp(draws), dims[dim] // blocks).reshape((-1,) + (1,) * (len(dims) - 1 - dim))
    return level


def centred(stream_key, dims, scale, bound, cuts=(), kind=jnp.bfloat16):
    gain = levels(stream_key, dims, cuts, -0.22, 0.18) if cuts else 1.0
    array = jax.random.normal(stream_key, dims, jnp.float32) * scale * gain
    return jnp.minimum(jnp.maximum(array, -bound), bound).astype(kind)


def setup_inputs(seed: int = 0) -> dict:
    key_of = jax.random.split(jax.random.key(seed), 7)
    inputs = centred(key_of[0], (SEQS, SEQLEN, D), 1.0, 6.0, ((0, 4), (1, 8)), jnp.float32)
    guess = jnp.clip(jax.random.uniform(key_of[1], (SEQS, SEQLEN, H), jnp.float32, -0.9, 0.9) * levels(key_of[1], (SEQS, SEQLEN, H), ((0, 4), (1, 8)), -0.4, 0.0), -0.9, 0.9)
    cotangent = centred(key_of[2], (SEQS, SEQLEN, H), 0.05, 0.4, ((0, 4), (1, 8)), jnp.float32)
    w_input = centred(key_of[3], (D, 3 * H), D ** -0.5, 0.75, (), jnp.float32)
    w_hidden = centred(key_of[4], (H, 3 * H), H ** -0.5, 0.75, (), jnp.float32)
    bias = draw_bias(jax.random.fold_in(key_of[6], 71), 0)
    return dict(inputs=inputs, guess=guess, cotangent=cotangent, w_input=w_input, w_hidden=w_hidden, bias=bias)


HIGHEST = lax.Precision.HIGHEST

def cell(inputs, prev, w_input, w_hidden, bias):
    width = prev.shape[-1]
    gate_in = jnp.einsum('...d,dk->...k', inputs, w_input, precision=HIGHEST) + bias[:3 * width]
    gate_hid = jnp.einsum('...j,jk->...k', prev, w_hidden, precision=HIGHEST)
    reset = jax.nn.sigmoid(gate_in[..., :width] + gate_hid[..., :width])
    update = jax.nn.sigmoid(gate_in[..., width:2 * width] + gate_hid[..., width:2 * width])
    hsum = gate_hid[..., 2 * width:] + bias[3 * width:]
    cand = jnp.tanh(gate_in[..., 2 * width:] + reset * hsum)
    value = (1.0 - update) * cand + update * prev
    return (value, (reset, update, cand, hsum))

def jacobian(prev, w_hidden, reset, update, cand, hsum):
    width = prev.shape[-1]
    w_reset = w_hidden[:, :width].T
    w_update = w_hidden[:, width:2 * width].T
    w_cand = w_hidden[:, 2 * width:].T
    squash = (1.0 - update) * (1.0 - cand * cand)
    coef_cand = squash * reset
    coef_reset = squash * hsum * reset * (1.0 - reset)
    coef_update = (prev - cand) * update * (1.0 - update)
    identity_mat = jnp.eye(width, dtype=jnp.float32)
    return coef_cand[..., :, None] * w_cand + coef_reset[..., :, None] * w_reset + coef_update[..., :, None] * w_update + update[..., :, None] * identity_mat

def reference(inputs, guess, cotangent, w_input, w_hidden, bias):
    prev = jnp.concatenate([jnp.zeros_like(guess[:, :1]), guess[:, :-1]], axis=1)
    value, parts = cell(inputs, prev, w_input, w_hidden, bias)
    series = tuple((jnp.moveaxis(a, 1, 0) for a in (prev, value, cotangent) + parts))

    def forward_step(state, items):
        prev_t, value_t, cot_t, reset, update, cand, hsum = items
        jac = jacobian(prev_t, w_hidden, reset, update, cand, hsum)
        shift = value_t - jnp.einsum('sij,sj->si', jac, prev_t, precision=HIGHEST)
        state = jnp.einsum('sij,sj->si', jac, state, precision=HIGHEST) + shift
        return (state, state)

    def backward_step(carry, items):
        prev_t, value_t, cot_t, reset, update, cand, hsum = items
        jac = jacobian(prev_t, w_hidden, reset, update, cand, hsum)
        lam = cot_t + carry
        carry = jnp.einsum('sji,sj->si', jac, lam, precision=HIGHEST)
        return (carry, lam)
    start = jnp.zeros_like(guess[:, 0])
    unused, states = lax.scan(forward_step, start, series)
    unused, lams = lax.scan(backward_step, start, series, reverse=True)
    new_states = jnp.moveaxis(states, 0, 1)
    adjoint = jnp.moveaxis(lams, 0, 1)
    unused, pullback = jax.vjp(lambda a, b, c: cell(inputs, prev, a, b, c)[0], w_input, w_hidden, bias)
    grad_a, grad_b, grad_c = pullback(adjoint)
    scale = 1.0 / math.sqrt(SEQS * SEQLEN)
    return (new_states, adjoint, grad_a * scale, grad_b * scale, grad_c * scale)
```

```python
import functools
import math

import jax
import jax.numpy as jnp
from jax import lax
from jax.experimental import pallas as pl
from jax.experimental.pallas import tpu as pltpu
from jax.sharding import PartitionSpec as P

HIGHEST = lax.Precision.HIGHEST
MESH = pl.DeviceIdType.MESH
F32 = jnp.float32
BF16 = jnp.bfloat16
RUN = 16


def dot(a, b):
    return jnp.dot(a, b, precision=HIGHEST, preferred_element_type=F32)


def dot_t(a, b):
    return lax.dot_general(
        a, b, (((1,), (1,)), ((), ())), precision=HIGHEST, preferred_element_type=F32
    )


def split(x):
    high = x.astype(BF16)
    return high, (x - high.astype(F32)).astype(BF16)


def pack(x):
    half = x.shape[0] // 2
    return jnp.concatenate([x[:half], x[half:]], axis=1)


def twice(w):
    zero = jnp.zeros_like(w)
    return jnp.concatenate(
        [jnp.concatenate([w, zero], axis=1), jnp.concatenate([zero, w], axis=1)], axis=0
    )


def join(early, late):
    a0, b0, c0 = early
    a1, b1, c1 = late
    return (dot(a0, a1), dot(b0, a1) + b1, dot_t(c1, a0) + c0)


def body(
    tm, seq, scale,
    x_ref, g_ref, c_ref, wi_ref, wh_ref, b_ref,
    ns_ref, adj_ref, gi_ref, gh_ref, gb_ref,
    halo, p_s, q_s, w_s, u_s, s_s, c_s, sq_s, lam_s, new_s, lhs_s,
    wh2_s, wl_s, wt_s, mat_s, off_s, acc_s, maps, grad_s, rs_s, seq_s, full_s,
    h_send, h_recv, m_send, m_recv, r_send, r_recv, q_send, q_recv, f_send, f_recv,
):
    me, my_seq = lax.axis_index("tm"), lax.axis_index("seq")
    steps, width = x_ref.shape[1], x_ref.shape[2]
    rows = steps // 2
    pairs = rows // RUN

    def peer(k):
        return lax.rem(me + k, tm)

    def seq_peer(k):
        return lax.rem(my_seq + k, seq)

    barrier = pltpu.get_barrier_semaphore()
    for k in range(1, tm):
        pl.semaphore_signal(barrier, inc=1, device_id=(my_seq, peer(k)), device_id_type=MESH)
    for k in range(1, seq):
        pl.semaphore_signal(barrier, inc=1, device_id=(seq_peer(k), me), device_id_type=MESH)

    guess = g_ref[0]
    halo[0] = jnp.concatenate([guess[steps - 8 :], guess[steps - 8 :]], axis=1)
    pl.semaphore_wait(barrier, tm + seq - 2)
    halo_copy = pltpu.make_async_remote_copy(
        halo.at[0], halo.at[1], h_send, h_recv, device_id=(my_seq, peer(1)), device_id_type=MESH
    )
    halo_copy.start()

    x = x_ref[0]
    wi, wh = wi_ref[...], wh_ref[...]

    def gates(w):
        return (w[:, 2 * width :], w[:, :width], w[:, width : 2 * width])

    big_i = jnp.concatenate([twice(w) for w in gates(wi)], axis=1)
    big_h = jnp.concatenate([twice(w) for w in gates(wh)], axis=1)
    high, low = split(big_h)
    wh2_s[...] = jnp.concatenate([high, high], axis=0)
    wl_s[...] = low
    back = jnp.concatenate([twice(w.T) for w in gates(wh)], axis=0)
    high, low = split(back)
    wt_s[...] = jnp.concatenate([high, low], axis=1)
    bias = b_ref[...]

    def bias_of(i):
        piece = bias[:, i * width : (i + 1) * width]
        return jnp.concatenate([piece, piece], axis=1)

    c_s[...] = pack(c_ref[0])
    gi = dot(pack(x), big_i)
    two = 2 * width

    halo_copy.wait()
    first = jnp.where(me > 0, halo[1][7:8, :width], 0.0)
    prev_full = jnp.concatenate([first, guess[: steps - 1]], axis=0)
    prev = pack(prev_full)
    lhs_s[...] = jnp.concatenate([x, prev_full], axis=1).T
    gh = dot(prev, big_h)
    ghn, ghr, ghz = gh[:, :two], gh[:, two : 2 * two], gh[:, 2 * two :]
    reset = jax.nn.sigmoid(gi[:, two : 2 * two] + bias_of(0) + ghr)
    update = jax.nn.sigmoid(gi[:, 2 * two :] + bias_of(1) + ghz)
    hsum = ghn + bias_of(3)
    cand = jnp.tanh(gi[:, :two] + bias_of(2) + reset * hsum)
    keep = 1.0 - update
    squash = keep * (1.0 - cand * cand)
    coef_p = squash * reset
    coef_q = coef_p * hsum * (1.0 - reset)
    coef_w = (prev - cand) * update * keep
    p_s[...], q_s[...], w_s[...], u_s[...], sq_s[...] = coef_p, coef_q, coef_w, update, squash
    s_s[...] = keep * cand - (coef_p * ghn + coef_q * ghr + coef_w * ghz)

    def at(ref, s):
        return ref[pl.ds(s, pairs, stride=RUN), :]

    def forward_dot(z):
        high, low = split(z)
        both = jnp.concatenate([high, low], axis=1)
        return jnp.dot(both, wh2_s[...], preferred_element_type=F32) + jnp.dot(
            high, wl_s[...], preferred_element_type=F32
        )

    eye = (
        lax.broadcasted_iota(jnp.int32, (width, two), 0)
        == lax.rem(lax.broadcasted_iota(jnp.int32, (width, two), 1), width)
    ).astype(F32)
    mat_s[...] = jnp.broadcast_to(eye[None], (pairs, width, two)).reshape(pairs * width, two)
    off_s[...] = jnp.zeros_like(off_s)
    acc_s[...] = jnp.zeros_like(acc_s)

    def group_step(s, carry):
        p, q, w, u = at(p_s, s), at(q_s, s), at(w_s, s), at(u_s, s)
        old = mat_s[...]
        y = forward_dot(old)
        shape = (pairs, width, two)
        new = (
            p[:, None, :] * y[:, :two].reshape(shape)
            + q[:, None, :] * y[:, two : 2 * two].reshape(shape)
            + w[:, None, :] * y[:, 2 * two :].reshape(shape)
            + u[:, None, :] * old.reshape(shape)
        )
        mat_s[...] = new.reshape(pairs * width, two)
        acc_s[...] += (new * at(c_s, s)[:, None, :]).reshape(pairs * width, two)
        off_s[...] = forward_vector(s, off_s[...])
        return carry

    def forward_vector(s, z):
        y = forward_dot(z)
        return (
            at(p_s, s) * y[:, :two]
            + at(q_s, s) * y[:, two : 2 * two]
            + at(w_s, s) * y[:, 2 * two :]
            + at(u_s, s) * z
            + at(s_s, s)
        )

    lax.fori_loop(0, RUN, group_step, 0)

    lane = lax.broadcasted_iota(jnp.int32, (width, two), 1)
    zeros = jnp.zeros((width, two), F32)

    def blocks(z):
        return jnp.concatenate(
            [jnp.where(lane < width, z, 0.0), jnp.where(lane < width, 0.0, z)], axis=0
        )

    def turn(z):
        return pltpu.roll(z, width, 1)

    def lower(z):
        return jnp.where(lane[: z.shape[0]] < width, z, 0.0)

    ones = jnp.ones((8, two), F32)
    level = []
    for j in range(pairs):
        rows_j = slice(j * width, (j + 1) * width)
        level.append((
            blocks(mat_s[rows_j, :]),
            jnp.broadcast_to(off_s[j : j + 1, :], (8, two)),
            dot_t(ones, blocks(acc_s[rows_j, :])),
        ))
    tree = [level]
    while len(level) > 1:
        level = [join(level[i], level[i + 1]) for i in range(0, len(level), 2)]
        tree.append(level)
    mat, off, coff = level[0]
    first_half = (jnp.concatenate([mat[:width], zeros], axis=0), lower(off), lower(coff))
    last_half = (
        jnp.concatenate([turn(mat[width:]), zeros], axis=0), lower(turn(off)), lower(turn(coff))
    )
    total, off, coff = join(first_half, last_half)
    half = width // 2
    maps[me] = jnp.concatenate(
        [total[:half] + turn(total[half:width]), off + turn(coff)], axis=0
    )
    copies = []
    for k in range(1, tm):
        copy = pltpu.make_async_remote_copy(
            maps.at[me], maps.at[me], m_send.at[k], m_recv.at[k],
            device_id=(my_seq, peer(k)), device_id_type=MESH,
        )
        copy.start()
        copies.append(copy)
    for copy in copies:
        copy.wait()

    def chain(d, carry):
        state, adj = carry
        other = tm - 1 - d

        def load(i):
            block = maps[i]
            mat = block[:half]
            mat = jnp.concatenate([lower(mat), lower(turn(mat)), zeros], axis=0)
            return mat, lower(block[half:]), lower(turn(block[half:]))

        mat, off, unused = load(d)
        state = jnp.where(d < me, dot(state, mat) + off, state)
        mat, unused, coff = load(other)
        adj = jnp.where(other > me, dot_t(adj, mat) + coff, adj)
        return state, adj

    zero = jnp.zeros((8, two), F32)
    state_in, adj_in = lax.fori_loop(0, tm, chain, (zero, zero))

    states = [state_in + turn(dot(state_in, first_half[0]) + first_half[1])]
    adjs = [dot_t(adj_in, last_half[0]) + last_half[2] + turn(adj_in)]
    for level in tree[-2::-1]:
        next_states, next_adjs = [], []
        for i in range(len(states)):
            (a0, b0, unused), (a1, unused, c1) = level[2 * i], level[2 * i + 1]
            next_states += [states[i], dot(states[i], a0) + b0]
            next_adjs += [dot_t(adjs[i], a1) + c1, adjs[i]]
        states, adjs = next_states, next_adjs

    def rows_of(parts):
        return jnp.concatenate([part[:1] for part in parts], axis=0)

    def adjoint_step(i, carry):
        s = RUN - 1 - i
        lam = at(c_s, s) + carry
        lam_s[pl.ds(s, pairs, stride=RUN), :] = lam
        d = jnp.concatenate([at(p_s, s) * lam, at(q_s, s) * lam, at(w_s, s) * lam], axis=1)
        d = jnp.concatenate([d, d], axis=0)
        low = d - d.astype(BF16).astype(F32)
        upper = lax.broadcasted_iota(jnp.int32, d.shape, 0) < pairs
        both = jnp.where(upper, d, low).astype(BF16)
        y = jnp.dot(both, wt_s[...], preferred_element_type=F32)
        return at(u_s, s) * lam + y[:pairs, :two] + y[:pairs, two:] + y[pairs:, :two]

    lax.fori_loop(0, RUN, adjoint_step, rows_of(adjs))

    lam = lam_s[...]
    adj_ref[0] = jnp.concatenate([lam[:, :width], lam[:, width:]], axis=0)
    parts = [q_s[...] * lam, w_s[...] * lam, sq_s[...] * lam, p_s[...] * lam]
    terms = jnp.concatenate(
        [
            jnp.concatenate([part[:, :width] for part in parts], axis=1),
            jnp.concatenate([part[:, width:] for part in parts], axis=1),
        ],
        axis=0,
    )
    grads = dot(lhs_s[...], terms)
    sums = jnp.sum(terms, axis=0, keepdims=True)
    grad_s[:two] = grads[:, :two]
    grad_s[two:] = grads[:, two:]
    row = lax.broadcasted_iota(jnp.int32, (8, width), 0)
    block = jnp.zeros((8, width), F32)
    for i in range(4):
        block = jnp.where(row == i, sums[:, i * width : (i + 1) * width], block)
    grad_s[two : two + 8, width:] = block

    piece = grad_s.shape[0] // tm
    copies = []
    for k in range(1, tm):
        copy = pltpu.make_async_remote_copy(
            grad_s.at[pl.ds(pl.multiple_of(peer(k) * piece, 8), piece)], rs_s.at[k],
            r_send.at[k], r_recv.at[k], device_id=(my_seq, peer(k)), device_id_type=MESH,
        )
        copy.start()
        copies.append(copy)

    def state_step(s, z):
        z = forward_vector(s, z)
        new_s[pl.ds(s, pairs, stride=RUN), :] = z
        return z

    lax.fori_loop(0, RUN, state_step, rows_of(states))
    new = new_s[...]
    ns_ref[0] = jnp.concatenate([new[:, :width], new[:, width:]], axis=0)

    for copy in copies:
        copy.wait()
    part = grad_s[pl.ds(pl.multiple_of(me * piece, 8), piece)]
    for k in range(1, tm):
        part = part + rs_s[k]
    seq_s[my_seq] = part
    copies = []
    for k in range(1, seq):
        copy = pltpu.make_async_remote_copy(
            seq_s.at[my_seq], seq_s.at[my_seq], q_send.at[k], q_recv.at[k],
            device_id=(seq_peer(k), me), device_id_type=MESH,
        )
        copy.start()
        copies.append(copy)
    for copy in copies:
        copy.wait()
    part = seq_s[0]
    for k in range(1, seq):
        part = part + seq_s[k]
    full_s[me] = part * scale
    copies = []
    for k in range(1, tm):
        copy = pltpu.make_async_remote_copy(
            full_s.at[me], full_s.at[me], f_send.at[k], f_recv.at[k],
            device_id=(my_seq, peer(k)), device_id_type=MESH,
        )
        copy.start()
        copies.append(copy)
    for copy in copies:
        copy.wait()
    whole = full_s[...].reshape(2 * two, two)
    gi_ref[...] = jnp.concatenate([whole[:width], whole[two : two + width, :width]], axis=1)
    gh_ref[...] = jnp.concatenate([whole[width:two], whole[two + width :, width:]], axis=1)
    gb_ref[...] = jnp.concatenate(
        [whole[two + i : two + i + 1, width:] for i in range(4)], axis=1
    )


def per_device(tm, seq, inputs, guess, cotangent, w_input, w_hidden, bias):
    unused, steps, width = guess.shape
    two = 2 * width
    rows = steps // 2
    pairs = rows // RUN
    scale = 1.0 / math.sqrt(seq * tm * steps)
    vmem = pltpu.VMEM
    dma = pltpu.SemaphoreType.DMA
    piece = 2 * two // tm
    new, adj, grad_i, grad_h, grad_b = pl.pallas_call(
        functools.partial(body, tm, seq, scale),
        out_shape=(
            jax.ShapeDtypeStruct(guess.shape, F32),
            jax.ShapeDtypeStruct(guess.shape, F32),
            jax.ShapeDtypeStruct(w_input.shape, F32),
            jax.ShapeDtypeStruct(w_hidden.shape, F32),
            jax.ShapeDtypeStruct((1, bias.shape[0]), F32),
        ),
        in_specs=[pl.BlockSpec(memory_space=vmem)] * 6,
        out_specs=(pl.BlockSpec(memory_space=vmem),) * 5,
        scratch_shapes=[
            vmem((2, 8, two), F32),
            *[vmem((rows, two), F32) for unused in range(9)],
            vmem((two, steps), F32),
            vmem((2 * two, 3 * two), BF16),
            vmem((two, 3 * two), BF16),
            vmem((3 * two, 2 * two), BF16),
            vmem((pairs * width, two), F32),
            vmem((pairs, two), F32),
            vmem((pairs * width, two), F32),
            vmem((tm, width // 2 + 8, two), F32),
            vmem((2 * two, two), F32),
            vmem((tm, piece, two), F32),
            vmem((seq, piece, two), F32),
            vmem((tm, piece, two), F32),
            dma, dma,
            dma((tm,)), dma((tm,)),
            dma((tm,)), dma((tm,)),
            dma((seq,)), dma((seq,)),
            dma((tm,)), dma((tm,)),
        ],
        compiler_params=pltpu.CompilerParams(
            collective_id=0, has_side_effects=True, vmem_limit_bytes=32 * 1024 * 1024
        ),
    )(inputs, guess, cotangent, w_input, w_hidden, bias.reshape(1, -1))
    return new, adj, grad_i, grad_h, grad_b.reshape(-1)


def solution(mesh):
    return jax.shard_map(
        functools.partial(per_device, mesh.shape["tm"], mesh.shape["seq"]),
        mesh=mesh,
        in_specs=(P("seq", "tm", None), P("seq", "tm", None), P("seq", "tm", None), P(), P(), P()),
        out_specs=(P("seq", "tm", None), P("seq", "tm", None), P(), P(), P()),
        check_vma=False,
    )
```

```python
import functools
import math

import jax
import jax.numpy as jnp
from jax import lax
from jax.experimental import pallas as pl
from jax.experimental.pallas import tpu as pltpu
from jax.sharding import PartitionSpec as P

MESH = pl.DeviceIdType.MESH
F32 = jnp.float32
BF16 = jnp.bfloat16
RUN = 16


def split(x):
    high = x.astype(BF16)
    return high, (x - high.astype(F32)).astype(BF16)


def stack(w):
    return jnp.concatenate(split(w), axis=0)


def mm(a, stacked):
    both = jnp.concatenate([a, a - a.astype(BF16).astype(F32)], axis=0).astype(BF16)
    both = jnp.concatenate([both, both], axis=1)
    y = jnp.dot(both, stacked, preferred_element_type=F32)
    return y[: a.shape[0]] + y[a.shape[0] :]


def pack(x):
    half = x.shape[1] // 2
    return jnp.concatenate([x[:, :half], x[:, half:]], axis=0).T


def unpack(x):
    x = x.T
    half = x.shape[0] // 2
    return jnp.concatenate([x[:half], x[half:]], axis=1)


def twice(w):
    zero = jnp.zeros_like(w)
    return jnp.concatenate(
        [jnp.concatenate([w, zero], axis=1), jnp.concatenate([zero, w], axis=1)], axis=0
    )


def join(early, late):
    a0, b0, c0 = early
    a1, b1, c1 = late
    y = mm(jnp.concatenate([a0, b0], axis=0), stack(a1))
    count = a0.shape[0]
    return (y[:count], y[count:] + b1, mm(c1, stack(a0.T)) + c0)


def body(
    tm, seq, scale,
    x_hbm, g_hbm, c_hbm, wi_hbm, wh_hbm, b_hbm,
    ns_ref, adj_ref, gi_ref, gh_ref, gb_ref,
    x_ref, g_ref, c_ref, wi_ref, wh_ref, b_ref, in_sem,
    halo, p_s, q_s, w_s, u_s, s_s, c_s, sq_s, lam_s, new_s, lhs_s,
    wh2_s, wt_s, mat_s, off_s, acc_s, maps, grad_s, rs_s, seq_s, full_s,
    h_send, h_recv, m_send, m_recv, r_send, r_recv, q_send, q_recv, f_send, f_recv,
):
    fetch = [
        pltpu.make_async_copy(source, target, in_sem.at[i])
        for i, (source, target) in enumerate(
            [(g_hbm, g_ref), (x_hbm, x_ref), (wi_hbm, wi_ref), (wh_hbm, wh_ref),
             (b_hbm, b_ref), (c_hbm, c_ref)]
        )
    ]
    for copy in fetch:
        copy.start()
    me, my_seq = lax.axis_index("tm"), lax.axis_index("seq")
    width, steps = x_ref.shape[1], x_ref.shape[2]
    rows = steps // 2
    pairs = rows // RUN

    def peer(k):
        return lax.rem(me + k, tm)

    def seq_peer(k):
        return lax.rem(my_seq + k, seq)

    barrier = pltpu.get_barrier_semaphore()
    for k in range(1, tm):
        pl.semaphore_signal(barrier, inc=1, device_id=(my_seq, peer(k)), device_id_type=MESH)
    for k in range(1, seq):
        pl.semaphore_signal(barrier, inc=1, device_id=(seq_peer(k), me), device_id_type=MESH)

    fetch[0].wait()
    guess = pack(g_ref[0])
    halo[0] = guess[rows - 8 :]
    pl.semaphore_wait(barrier, tm + seq - 2)
    halo_copy = pltpu.make_async_remote_copy(
        halo.at[0], halo.at[1], h_send, h_recv, device_id=(my_seq, peer(1)), device_id_type=MESH
    )
    halo_copy.start()
    for copy in fetch[1:]:
        copy.wait()

    two = 2 * width
    x = x_ref[0]
    wi, wh = wi_ref[...], wh_ref[...]
    lane = lax.broadcasted_iota(jnp.int32, (width, two), 1)
    zeros = jnp.zeros((width, two), F32)

    def turn(z):
        return pltpu.roll(z, width, 1)

    def lower(z):
        return jnp.where(lane[: z.shape[0]] < width, z, 0.0)

    def gates(w):
        return (w[:, 2 * width :], w[:, :width], w[:, width : 2 * width])

    big_i = jnp.concatenate([twice(w) for w in gates(wi)], axis=1)
    big_h = jnp.concatenate([twice(w) for w in gates(wh)], axis=1)
    wh2_s[...] = stack(big_h)
    back = jnp.concatenate([twice(w.T) for w in gates(wh)], axis=0)
    high, low = split(back)
    wt_s[...] = jnp.concatenate([high, low], axis=1)
    bias = b_ref[...]

    def bias_of(i):
        piece = bias[:, i * width : (i + 1) * width]
        return jnp.concatenate([piece, piece], axis=1)

    c_s[...] = pack(c_ref[0])
    gi = mm(pack(x), stack(big_i))

    halo_copy.wait()
    first = jnp.where(me > 0, lower(turn(halo[1])), 0.0)[7:8]
    first = first + jnp.where(lane[:1] < width, 0.0, turn(guess[rows - 8 :])[7:8])
    prev = jnp.concatenate([first, guess[: rows - 1]], axis=0)
    lhs_s[...] = jnp.concatenate([x, unpack(prev)], axis=0)
    gh = mm(prev, wh2_s[...])
    ghn, ghr, ghz = gh[:, :two], gh[:, two : 2 * two], gh[:, 2 * two :]
    reset = jax.nn.sigmoid(gi[:, two : 2 * two] + bias_of(0) + ghr)
    update = jax.nn.sigmoid(gi[:, 2 * two :] + bias_of(1) + ghz)
    hsum = ghn + bias_of(3)
    cand = jnp.tanh(gi[:, :two] + bias_of(2) + reset * hsum)
    keep = 1.0 - update
    squash = keep * (1.0 - cand * cand)
    coef_p = squash * reset
    coef_q = coef_p * hsum * (1.0 - reset)
    coef_w = (prev - cand) * update * keep
    p_s[...], q_s[...], w_s[...], u_s[...], sq_s[...] = coef_p, coef_q, coef_w, update, squash
    s_s[...] = keep * cand - (coef_p * ghn + coef_q * ghr + coef_w * ghz)

    def at(ref, s):
        return ref[pl.ds(s, pairs, stride=RUN), :]

    shape = (pairs, width, two)
    flat = (pairs * width, two)
    wide = (lane % width == lax.broadcasted_iota(jnp.int32, (width, two), 0)).astype(F32)

    def tiled(w):
        return jnp.concatenate([w, w], axis=1)[None]

    def mixed(s, yn, yr, yz, old):
        return (
            at(p_s, s)[:, None, :] * yn
            + at(q_s, s)[:, None, :] * yr
            + at(w_s, s)[:, None, :] * yz
            + at(u_s, s)[:, None, :] * old
        )

    first = mixed(0, *[tiled(w) for w in gates(wh)], wide[None])
    mat_s[0] = first.reshape(flat)
    acc_s[...] = (first * at(c_s, 0)[:, None, :]).reshape(flat)
    off_s[0] = at(s_s, 0)

    def group_step(s, carry):
        old, off = mat_s[s - 1], off_s[s - 1]
        lhs = jnp.concatenate([old, off, off - off.astype(BF16).astype(F32)], axis=0).astype(BF16)
        y = jnp.dot(
            jnp.concatenate([lhs, lhs], axis=1), wh2_s[...], preferred_element_type=F32
        )
        mats, offs = y[: pairs * width], y[pairs * width :]
        offs = offs[:pairs] + offs[pairs:]
        new = mixed(
            s,
            mats[:, :two].reshape(shape),
            mats[:, two : 2 * two].reshape(shape),
            mats[:, 2 * two :].reshape(shape),
            old.reshape(shape),
        )
        mat_s[s] = new.reshape(flat)
        acc_s[...] += (new * at(c_s, s)[:, None, :]).reshape(flat)
        off_s[s] = (
            at(p_s, s) * offs[:, :two]
            + at(q_s, s) * offs[:, two : 2 * two]
            + at(w_s, s) * offs[:, 2 * two :]
            + at(u_s, s) * off
            + at(s_s, s)
        )
        return carry

    lax.fori_loop(1, RUN, group_step, 0)

    def spread(z):
        row = lax.broadcasted_iota(jnp.int32, (2 * two, two), 0) % two // width
        column = lax.broadcasted_iota(jnp.int32, (2 * two, two), 1) // width
        ones = (row == column).astype(BF16)
        return jnp.dot(jnp.concatenate(split(z), axis=1), ones, preferred_element_type=F32)

    def blocks(z):
        return jnp.concatenate(
            [jnp.where(lane < width, z, 0.0), jnp.where(lane < width, 0.0, z)], axis=0
        )

    sums = spread(acc_s[...]).reshape(shape) * wide[None]
    last, last_off = mat_s[RUN - 1], off_s[RUN - 1]
    level = []
    for j in range(pairs):
        level.append((
            blocks(last[j * width : (j + 1) * width]),
            jnp.broadcast_to(last_off[j : j + 1], (8, two)),
            jnp.broadcast_to(jnp.sum(sums[j], axis=0, keepdims=True), (8, two)),
        ))
    tree = [level]
    while len(level) > 1:
        level = [join(level[i], level[i + 1]) for i in range(0, len(level), 2)]
        tree.append(level)
    mat, off, coff = level[0]
    first_half = (jnp.concatenate([mat[:width], zeros], axis=0), lower(off), lower(coff))
    last_half = (
        jnp.concatenate([turn(mat[width:]), zeros], axis=0), lower(turn(off)), lower(turn(coff))
    )
    total, off, coff = join(first_half, last_half)
    half = width // 2
    maps[me] = jnp.concatenate(
        [total[:half] + turn(total[half:width]), off + turn(coff)], axis=0
    )
    copies = []
    for k in range(1, tm):
        copy = pltpu.make_async_remote_copy(
            maps.at[me], maps.at[me], m_send.at[k], m_recv.at[k],
            device_id=(my_seq, peer(k)), device_id_type=MESH,
        )
        copy.start()
        copies.append(copy)
    for copy in copies:
        copy.wait()

    def chain(d, carry):
        state, adj = carry
        other = tm - 1 - d

        def load(i):
            block = maps[i]
            mat = block[:half]
            mat = jnp.concatenate([lower(mat), lower(turn(mat)), zeros], axis=0)
            return mat, lower(block[half:]), lower(turn(block[half:]))

        mat, off, unused = load(d)
        state = jnp.where(d < me, mm(state, stack(mat)) + off, state)
        mat, unused, coff = load(other)
        adj = jnp.where(other > me, mm(adj, stack(mat.T)) + coff, adj)
        return state, adj

    zero = jnp.zeros((8, two), F32)
    state_in, adj_in = lax.fori_loop(0, tm, chain, (zero, zero), unroll=True)

    states = [state_in + turn(mm(state_in, stack(first_half[0])) + first_half[1])]
    adjs = [mm(adj_in, stack(last_half[0].T)) + last_half[2] + turn(adj_in)]
    for level in tree[-2::-1]:
        next_states, next_adjs = [], []
        for i in range(len(states)):
            (a0, b0, unused), (a1, unused, c1) = level[2 * i], level[2 * i + 1]
            next_states += [states[i], mm(states[i], stack(a0)) + b0]
            next_adjs += [mm(adjs[i], stack(a1.T)) + c1, adjs[i]]
        states, adjs = next_states, next_adjs

    def rows_of(parts):
        return jnp.concatenate([part[:1] for part in parts], axis=0)

    def adjoint_step(i, carry):
        s = RUN - 1 - i
        lam = at(c_s, s) + carry
        lam_s[pl.ds(s, pairs, stride=RUN), :] = lam
        d = jnp.concatenate([at(p_s, s) * lam, at(q_s, s) * lam, at(w_s, s) * lam], axis=1)
        d = jnp.concatenate([d, d], axis=0)
        low = d - d.astype(BF16).astype(F32)
        upper = lax.broadcasted_iota(jnp.int32, d.shape, 0) < pairs
        both = jnp.where(upper, d, low).astype(BF16)
        y = jnp.dot(both, wt_s[...], preferred_element_type=F32)
        return at(u_s, s) * lam + y[:pairs, :two] + y[:pairs, two:] + y[pairs:, :two]

    lax.fori_loop(0, RUN, adjoint_step, rows_of(adjs))

    lam = lam_s[...]
    adj_ref[0] = unpack(lam)
    parts = [q_s[...] * lam, w_s[...] * lam, sq_s[...] * lam, p_s[...] * lam]
    terms = jnp.concatenate(
        [
            jnp.concatenate([part[:, :width] for part in parts], axis=1),
            jnp.concatenate([part[:, width:] for part in parts], axis=1),
        ],
        axis=0,
    )
    grads = mm(lhs_s[...], stack(terms))
    sums = jnp.sum(terms, axis=0, keepdims=True)
    grad_s[:two] = grads[:, :two]
    grad_s[two:] = grads[:, two:]
    row = lax.broadcasted_iota(jnp.int32, (8, width), 0)
    block = jnp.zeros((8, width), F32)
    for i in range(4):
        block = jnp.where(row == i, sums[:, i * width : (i + 1) * width], block)
    grad_s[two : two + 8, width:] = block

    piece = grad_s.shape[0] // tm
    copies = []
    for k in range(1, tm):
        copy = pltpu.make_async_remote_copy(
            grad_s.at[pl.ds(pl.multiple_of(peer(k) * piece, 8), piece)], rs_s.at[k],
            r_send.at[k], r_recv.at[k], device_id=(my_seq, peer(k)), device_id_type=MESH,
        )
        copy.start()
        copies.append(copy)

    starts = spread(
        (jnp.concatenate([z[:1][None] for z in states], axis=0) * wide[None]).reshape(flat)
    ).reshape(shape)

    def state_step(s, carry):
        moved = jnp.sum(mat_s[s].reshape(shape) * starts, axis=1)
        new_s[pl.ds(s, pairs, stride=RUN), :] = moved + off_s[s]
        return carry

    lax.fori_loop(0, RUN, state_step, 0)
    ns_ref[0] = unpack(new_s[...])

    for copy in copies:
        copy.wait()
    part = grad_s[pl.ds(pl.multiple_of(me * piece, 8), piece)]
    for k in range(1, tm):
        part = part + rs_s[k]
    seq_s[my_seq] = part
    copies = []
    for k in range(1, seq):
        copy = pltpu.make_async_remote_copy(
            seq_s.at[my_seq], seq_s.at[my_seq], q_send.at[k], q_recv.at[k],
            device_id=(seq_peer(k), me), device_id_type=MESH,
        )
        copy.start()
        copies.append(copy)
    for copy in copies:
        copy.wait()
    part = seq_s[0]
    for k in range(1, seq):
        part = part + seq_s[k]
    full_s[me] = part * scale
    copies = []
    for k in range(1, tm):
        copy = pltpu.make_async_remote_copy(
            full_s.at[me], full_s.at[me], f_send.at[k], f_recv.at[k],
            device_id=(my_seq, peer(k)), device_id_type=MESH,
        )
        copy.start()
        copies.append(copy)
    for copy in copies:
        copy.wait()
    whole = full_s[...].reshape(2 * two, two)
    gi_ref[...] = jnp.concatenate([whole[:width], whole[two : two + width, :width]], axis=1)
    gh_ref[...] = jnp.concatenate([whole[width:two], whole[two + width :, width:]], axis=1)
    gb_ref[...] = jnp.concatenate(
        [whole[two + i : two + i + 1, width:] for i in range(4)], axis=1
    )


def finish(a0, a1, a2, a3, a4, b0, b1, b2, b3, b4, sem):
    copies = [
        pltpu.make_async_copy(source, target, sem.at[i])
        for i, (source, target) in enumerate(
            [(a0, b0), (a1, b1), (a2, b2), (a3, b3), (a4, b4)]
        )
    ]
    for copy in copies:
        copy.start()
    for copy in copies:
        copy.wait()


def per_device(tm, seq, inputs, guess, cotangent, w_input, w_hidden, bias):
    unused, steps, width = guess.shape
    two = 2 * width
    rows = steps // 2
    pairs = rows // RUN
    scale = 1.0 / math.sqrt(seq * tm * steps)
    vmem = pltpu.VMEM
    dma = pltpu.SemaphoreType.DMA
    piece = 2 * two // tm
    turned = (guess.shape[0], width, steps)
    arrays = [jnp.swapaxes(z, 1, 2) for z in (inputs, guess, cotangent)]
    arrays += [w_input, w_hidden, bias.reshape(1, -1)]
    outs = (
        jax.ShapeDtypeStruct(turned, F32),
        jax.ShapeDtypeStruct(turned, F32),
        jax.ShapeDtypeStruct(w_input.shape, F32),
        jax.ShapeDtypeStruct(w_hidden.shape, F32),
        jax.ShapeDtypeStruct((1, bias.shape[0]), F32),
    )
    results = pl.pallas_call(
        functools.partial(body, tm, seq, scale),
        out_shape=outs,
        in_specs=[pl.BlockSpec(memory_space=pltpu.HBM)] * 6,
        out_specs=(pl.BlockSpec(memory_space=vmem),) * 5,
        scratch_shapes=[
            *[vmem(z.shape, F32) for z in arrays],
            dma((6,)),
            vmem((2, 8, two), F32),
            *[vmem((rows, two), F32) for unused in range(9)],
            vmem((two, steps), F32),
            vmem((2 * two, 3 * two), BF16),
            vmem((3 * two, 2 * two), BF16),
            vmem((RUN, pairs * width, two), F32),
            vmem((RUN, pairs, two), F32),
            vmem((pairs * width, two), F32),
            vmem((tm, width // 2 + 8, two), F32),
            vmem((2 * two, two), F32),
            vmem((tm, piece, two), F32),
            vmem((seq, piece, two), F32),
            vmem((tm, piece, two), F32),
            dma, dma,
            dma((tm,)), dma((tm,)),
            dma((tm,)), dma((tm,)),
            dma((seq,)), dma((seq,)),
            dma((tm,)), dma((tm,)),
        ],
        compiler_params=pltpu.CompilerParams(
            collective_id=0, has_side_effects=True, vmem_limit_bytes=48 * 1024 * 1024
        ),
    )(*arrays)
    new, adj, grad_i, grad_h, grad_b = pl.pallas_call(
        finish,
        out_shape=outs,
        in_specs=[pl.BlockSpec(memory_space=vmem)] * 5,
        out_specs=(pl.BlockSpec(memory_space=pl.ANY),) * 5,
        scratch_shapes=[dma((5,))],
    )(*results)
    return jnp.swapaxes(new, 1, 2), jnp.swapaxes(adj, 1, 2), grad_i, grad_h, grad_b.reshape(-1)


def solution(mesh):
    return jax.shard_map(
        functools.partial(per_device, mesh.shape["tm"], mesh.shape["seq"]),
        mesh=mesh,
        in_specs=(P("seq", "tm", None), P("seq", "tm", None), P("seq", "tm", None), P(), P(), P()),
        out_specs=(P("seq", "tm", None), P("seq", "tm", None), P(), P(), P()),
        check_vma=False,
    )
```

```python
import functools
import math

import jax
import jax.numpy as jnp
from jax import lax
from jax.experimental import pallas as pl
from jax.experimental.pallas import tpu as pltpu
from jax.sharding import PartitionSpec as P

MESH = pl.DeviceIdType.MESH
F32 = jnp.float32
BF16 = jnp.bfloat16
RUN = 8


def split(x):
    high = x.astype(BF16)
    return high, (x - high.astype(F32)).astype(BF16)


def stack(w):
    return jnp.concatenate(split(w), axis=0)


def mm(a, stacked):
    both = jnp.concatenate([a, a - a.astype(BF16).astype(F32)], axis=0).astype(BF16)
    both = jnp.concatenate([both, both], axis=1)
    y = jnp.dot(both, stacked, preferred_element_type=F32)
    return y[: a.shape[0]] + y[a.shape[0] :]


def pack(x):
    half = x.shape[1] // 2
    return jnp.concatenate([x[:, :half], x[:, half:]], axis=0).T


def unpack(x):
    x = x.T
    half = x.shape[0] // 2
    return jnp.concatenate([x[:half], x[half:]], axis=1)


def twice(w):
    zero = jnp.zeros_like(w)
    return jnp.concatenate(
        [jnp.concatenate([w, zero], axis=1), jnp.concatenate([zero, w], axis=1)], axis=0
    )


def join(early, late):
    a0, b0, c0 = early
    a1, b1, c1 = late
    y = mm(jnp.concatenate([a0, b0], axis=0), stack(a1))
    count = a0.shape[0]
    return (y[:count], y[count:] + b1, mm(c1, stack(a0.T)) + c0)


def body(
    tm, seq, scale,
    x_hbm, g_hbm, c_hbm, wi_hbm, wh_hbm, b_hbm,
    ns_ref, adj_ref, gi_ref, gh_ref, gb_ref,
    x_ref, g_ref, c_ref, wi_ref, wh_ref, b_ref, in_sem,
    halo, p_s, q_s, w_s, u_s, s_s, c_s, sq_s, lam_s, new_s, lhs_s,
    wh2_s, wt_s, mat_s, off_s, acc_s, maps, grad_s, rs_s, seq_s, full_s,
    h_send, h_recv, m_send, m_recv, r_send, r_recv, q_send, q_recv, f_send, f_recv,
):
    fetch = [
        pltpu.make_async_copy(source, target, in_sem.at[i])
        for i, (source, target) in enumerate(
            [(g_hbm, g_ref), (x_hbm, x_ref), (wi_hbm, wi_ref), (wh_hbm, wh_ref),
             (b_hbm, b_ref), (c_hbm, c_ref)]
        )
    ]
    for copy in fetch:
        copy.start()
    me, my_seq = lax.axis_index("tm"), lax.axis_index("seq")
    width, steps = x_ref.shape[1], x_ref.shape[2]
    rows = steps // 2
    pairs = rows // RUN

    def peer(k):
        return lax.rem(me + k, tm)

    def seq_peer(k):
        return lax.rem(my_seq + k, seq)

    barrier = pltpu.get_barrier_semaphore()
    for k in range(1, tm):
        pl.semaphore_signal(barrier, inc=1, device_id=(my_seq, peer(k)), device_id_type=MESH)
    for k in range(1, seq):
        pl.semaphore_signal(barrier, inc=1, device_id=(seq_peer(k), me), device_id_type=MESH)

    fetch[0].wait()
    guess = pack(g_ref[0])
    halo[0] = guess[rows - 8 :]
    pl.semaphore_wait(barrier, tm + seq - 2)
    halo_copy = pltpu.make_async_remote_copy(
        halo.at[0], halo.at[1], h_send, h_recv, device_id=(my_seq, peer(1)), device_id_type=MESH
    )
    halo_copy.start()
    for copy in fetch[1:]:
        copy.wait()

    two = 2 * width
    x = x_ref[0]
    wi, wh = wi_ref[...], wh_ref[...]
    lane = lax.broadcasted_iota(jnp.int32, (width, two), 1)
    zeros = jnp.zeros((width, two), F32)

    def turn(z):
        return pltpu.roll(z, width, 1)

    def lower(z):
        return jnp.where(lane[: z.shape[0]] < width, z, 0.0)

    def gates(w):
        return (w[:, 2 * width :], w[:, :width], w[:, width : 2 * width])

    big_i = jnp.concatenate([twice(w) for w in gates(wi)], axis=1)
    big_h = jnp.concatenate([twice(w) for w in gates(wh)], axis=1)
    wh2_s[...] = stack(big_h)
    back = jnp.concatenate([twice(w.T) for w in gates(wh)], axis=0)
    high, low = split(back)
    wt_s[...] = jnp.concatenate([high, low], axis=1)
    bias = b_ref[...]

    def bias_of(i):
        piece = bias[:, i * width : (i + 1) * width]
        return jnp.concatenate([piece, piece], axis=1)

    c_s[...] = pack(c_ref[0])
    gi = mm(pack(x), stack(big_i))

    halo_copy.wait()
    first = jnp.where(me > 0, lower(turn(halo[1])), 0.0)[7:8]
    first = first + jnp.where(lane[:1] < width, 0.0, turn(guess[rows - 8 :])[7:8])
    prev = jnp.concatenate([first, guess[: rows - 1]], axis=0)
    lhs_s[...] = jnp.concatenate([x, unpack(prev)], axis=0)
    gh = mm(prev, wh2_s[...])
    ghn, ghr, ghz = gh[:, :two], gh[:, two : 2 * two], gh[:, 2 * two :]
    reset = jax.nn.sigmoid(gi[:, two : 2 * two] + bias_of(0) + ghr)
    update = jax.nn.sigmoid(gi[:, 2 * two :] + bias_of(1) + ghz)
    hsum = ghn + bias_of(3)
    cand = jnp.tanh(gi[:, :two] + bias_of(2) + reset * hsum)
    keep = 1.0 - update
    squash = keep * (1.0 - cand * cand)
    coef_p = squash * reset
    coef_q = coef_p * hsum * (1.0 - reset)
    coef_w = (prev - cand) * update * keep
    p_s[...], q_s[...], w_s[...], u_s[...], sq_s[...] = coef_p, coef_q, coef_w, update, squash
    s_s[...] = keep * cand - (coef_p * ghn + coef_q * ghr + coef_w * ghz)

    def at(ref, s):
        return ref[pl.ds(s, pairs, stride=RUN), :]

    shape = (pairs, width, two)
    flat = (pairs * width, two)
    wide = (lane % width == lax.broadcasted_iota(jnp.int32, (width, two), 0)).astype(F32)

    def tiled(w):
        return jnp.concatenate([w, w], axis=1)[None]

    def mixed(s, yn, yr, yz, old):
        return (
            at(p_s, s)[:, None, :] * yn
            + at(q_s, s)[:, None, :] * yr
            + at(w_s, s)[:, None, :] * yz
            + at(u_s, s)[:, None, :] * old
        )

    first = mixed(0, *[tiled(w) for w in gates(wh)], wide[None])
    mat_s[0] = first.reshape(flat)
    acc_s[...] = (first * at(c_s, 0)[:, None, :]).reshape(flat)
    off_s[0] = at(s_s, 0)

    def group_step(s, carry):
        old, off = mat_s[s - 1], off_s[s - 1]
        lhs = jnp.concatenate([old, off, off - off.astype(BF16).astype(F32)], axis=0).astype(BF16)
        y = jnp.dot(
            jnp.concatenate([lhs, lhs], axis=1), wh2_s[...], preferred_element_type=F32
        )
        mats, offs = y[: pairs * width], y[pairs * width :]
        offs = offs[:pairs] + offs[pairs:]
        new = mixed(
            s,
            mats[:, :two].reshape(shape),
            mats[:, two : 2 * two].reshape(shape),
            mats[:, 2 * two :].reshape(shape),
            old.reshape(shape),
        )
        mat_s[s] = new.reshape(flat)
        acc_s[...] += (new * at(c_s, s)[:, None, :]).reshape(flat)
        off_s[s] = (
            at(p_s, s) * offs[:, :two]
            + at(q_s, s) * offs[:, two : 2 * two]
            + at(w_s, s) * offs[:, 2 * two :]
            + at(u_s, s) * off
            + at(s_s, s)
        )
        return carry

    lax.fori_loop(1, RUN, group_step, 0)

    def spread(z):
        row = lax.broadcasted_iota(jnp.int32, (2 * two, two), 0) % two // width
        column = lax.broadcasted_iota(jnp.int32, (2 * two, two), 1) // width
        ones = (row == column).astype(BF16)
        return jnp.dot(jnp.concatenate(split(z), axis=1), ones, preferred_element_type=F32)

    def blocks(z):
        return jnp.concatenate(
            [jnp.where(lane < width, z, 0.0), jnp.where(lane < width, 0.0, z)], axis=0
        )

    sums = spread(acc_s[...]).reshape(shape) * wide[None]
    last, last_off = mat_s[RUN - 1], off_s[RUN - 1]
    level = []
    for j in range(pairs):
        level.append((
            blocks(last[j * width : (j + 1) * width]),
            jnp.broadcast_to(last_off[j : j + 1], (8, two)),
            jnp.broadcast_to(jnp.sum(sums[j], axis=0, keepdims=True), (8, two)),
        ))
    tree = [level]
    while len(level) > 1:
        level = [join(level[i], level[i + 1]) for i in range(0, len(level), 2)]
        tree.append(level)
    mat, off, coff = level[0]
    first_half = (jnp.concatenate([mat[:width], zeros], axis=0), lower(off), lower(coff))
    last_half = (
        jnp.concatenate([turn(mat[width:]), zeros], axis=0), lower(turn(off)), lower(turn(coff))
    )
    total, off, coff = join(first_half, last_half)
    half = width // 2
    maps[me] = jnp.concatenate(
        [total[:half] + turn(total[half:width]), off + turn(coff)], axis=0
    )
    copies = []
    for k in range(1, tm):
        copy = pltpu.make_async_remote_copy(
            maps.at[me], maps.at[me], m_send.at[k], m_recv.at[k],
            device_id=(my_seq, peer(k)), device_id_type=MESH,
        )
        copy.start()
        copies.append(copy)
    for copy in copies:
        copy.wait()

    def chain(d, carry):
        state, adj = carry
        other = tm - 1 - d

        def load(i):
            block = maps[i]
            mat = block[:half]
            mat = jnp.concatenate([lower(mat), lower(turn(mat)), zeros], axis=0)
            return mat, lower(block[half:]), lower(turn(block[half:]))

        mat, off, unused = load(d)
        state = jnp.where(d < me, mm(state, stack(mat)) + off, state)
        mat, unused, coff = load(other)
        adj = jnp.where(other > me, mm(adj, stack(mat.T)) + coff, adj)
        return state, adj

    zero = jnp.zeros((8, two), F32)
    state_in, adj_in = lax.fori_loop(0, tm, chain, (zero, zero), unroll=True)

    states = [state_in + turn(mm(state_in, stack(first_half[0])) + first_half[1])]
    adjs = [mm(adj_in, stack(last_half[0].T)) + last_half[2] + turn(adj_in)]
    for level in tree[-2::-1]:
        next_states, next_adjs = [], []
        for i in range(len(states)):
            (a0, b0, unused), (a1, unused, c1) = level[2 * i], level[2 * i + 1]
            next_states += [states[i], mm(states[i], stack(a0)) + b0]
            next_adjs += [mm(adjs[i], stack(a1.T)) + c1, adjs[i]]
        states, adjs = next_states, next_adjs

    def rows_of(parts):
        return jnp.concatenate([part[:1] for part in parts], axis=0)

    def adjoint_step(i, carry):
        s = RUN - 1 - i
        lam = at(c_s, s) + carry
        lam_s[pl.ds(s, pairs, stride=RUN), :] = lam
        d = jnp.concatenate([at(p_s, s) * lam, at(q_s, s) * lam, at(w_s, s) * lam], axis=1)
        d = jnp.concatenate([d, d], axis=0)
        low = d - d.astype(BF16).astype(F32)
        upper = lax.broadcasted_iota(jnp.int32, d.shape, 0) < pairs
        both = jnp.where(upper, d, low).astype(BF16)
        y = jnp.dot(both, wt_s[...], preferred_element_type=F32)
        return at(u_s, s) * lam + y[:pairs, :two] + y[:pairs, two:] + y[pairs:, :two]

    lax.fori_loop(0, RUN, adjoint_step, rows_of(adjs))

    lam = lam_s[...]
    adj_ref[0] = unpack(lam)
    parts = [q_s[...] * lam, w_s[...] * lam, sq_s[...] * lam, p_s[...] * lam]
    terms = jnp.concatenate(
        [
            jnp.concatenate([part[:, :width] for part in parts], axis=1),
            jnp.concatenate([part[:, width:] for part in parts], axis=1),
        ],
        axis=0,
    )
    grads = mm(lhs_s[...], stack(terms))
    sums = jnp.sum(terms, axis=0, keepdims=True)
    grad_s[:two] = grads[:, :two]
    grad_s[two:] = grads[:, two:]
    row = lax.broadcasted_iota(jnp.int32, (8, width), 0)
    block = jnp.zeros((8, width), F32)
    for i in range(4):
        block = jnp.where(row == i, sums[:, i * width : (i + 1) * width], block)
    grad_s[two : two + 8, width:] = block

    piece = grad_s.shape[0] // tm
    copies = []
    for k in range(1, tm):
        copy = pltpu.make_async_remote_copy(
            grad_s.at[pl.ds(pl.multiple_of(peer(k) * piece, 8), piece)], rs_s.at[k],
            r_send.at[k], r_recv.at[k], device_id=(my_seq, peer(k)), device_id_type=MESH,
        )
        copy.start()
        copies.append(copy)

    starts = spread(
        (jnp.concatenate([z[:1][None] for z in states], axis=0) * wide[None]).reshape(flat)
    ).reshape(shape)

    def state_step(s, carry):
        moved = jnp.sum(mat_s[s].reshape(shape) * starts, axis=1)
        new_s[pl.ds(s, pairs, stride=RUN), :] = moved + off_s[s]
        return carry

    lax.fori_loop(0, RUN, state_step, 0)
    ns_ref[0] = unpack(new_s[...])

    for copy in copies:
        copy.wait()
    part = grad_s[pl.ds(pl.multiple_of(me * piece, 8), piece)]
    for k in range(1, tm):
        part = part + rs_s[k]
    seq_s[my_seq] = part
    copies = []
    for k in range(1, seq):
        copy = pltpu.make_async_remote_copy(
            seq_s.at[my_seq], seq_s.at[my_seq], q_send.at[k], q_recv.at[k],
            device_id=(seq_peer(k), me), device_id_type=MESH,
        )
        copy.start()
        copies.append(copy)
    for copy in copies:
        copy.wait()
    part = seq_s[0]
    for k in range(1, seq):
        part = part + seq_s[k]
    full_s[me] = part * scale
    copies = []
    for k in range(1, tm):
        copy = pltpu.make_async_remote_copy(
            full_s.at[me], full_s.at[me], f_send.at[k], f_recv.at[k],
            device_id=(my_seq, peer(k)), device_id_type=MESH,
        )
        copy.start()
        copies.append(copy)
    for copy in copies:
        copy.wait()
    whole = full_s[...].reshape(2 * two, two)
    gi_ref[...] = jnp.concatenate([whole[:width], whole[two : two + width, :width]], axis=1)
    gh_ref[...] = jnp.concatenate([whole[width:two], whole[two + width :, width:]], axis=1)
    gb_ref[...] = jnp.concatenate(
        [whole[two + i : two + i + 1, width:] for i in range(4)], axis=1
    )


def finish(a0, a1, a2, a3, a4, b0, b1, b2, b3, b4, sem):
    copies = [
        pltpu.make_async_copy(source, target, sem.at[i])
        for i, (source, target) in enumerate(
            [(a0, b0), (a1, b1), (a2, b2), (a3, b3), (a4, b4)]
        )
    ]
    for copy in copies:
        copy.start()
    for copy in copies:
        copy.wait()


def per_device(tm, seq, inputs, guess, cotangent, w_input, w_hidden, bias):
    unused, steps, width = guess.shape
    two = 2 * width
    rows = steps // 2
    pairs = rows // RUN
    scale = 1.0 / math.sqrt(seq * tm * steps)
    vmem = pltpu.VMEM
    dma = pltpu.SemaphoreType.DMA
    piece = 2 * two // tm
    turned = (guess.shape[0], width, steps)
    arrays = [jnp.swapaxes(z, 1, 2) for z in (inputs, guess, cotangent)]
    arrays += [w_input, w_hidden, bias.reshape(1, -1)]
    outs = (
        jax.ShapeDtypeStruct(turned, F32),
        jax.ShapeDtypeStruct(turned, F32),
        jax.ShapeDtypeStruct(w_input.shape, F32),
        jax.ShapeDtypeStruct(w_hidden.shape, F32),
        jax.ShapeDtypeStruct((1, bias.shape[0]), F32),
    )
    results = pl.pallas_call(
        functools.partial(body, tm, seq, scale),
        out_shape=outs,
        in_specs=[pl.BlockSpec(memory_space=pltpu.HBM)] * 6,
        out_specs=(pl.BlockSpec(memory_space=vmem),) * 5,
        scratch_shapes=[
            *[vmem(z.shape, F32) for z in arrays],
            dma((6,)),
            vmem((2, 8, two), F32),
            *[vmem((rows, two), F32) for unused in range(9)],
            vmem((two, steps), F32),
            vmem((2 * two, 3 * two), BF16),
            vmem((3 * two, 2 * two), BF16),
            vmem((RUN, pairs * width, two), F32),
            vmem((RUN, pairs, two), F32),
            vmem((pairs * width, two), F32),
            vmem((tm, width // 2 + 8, two), F32),
            vmem((2 * two, two), F32),
            vmem((tm, piece, two), F32),
            vmem((seq, piece, two), F32),
            vmem((tm, piece, two), F32),
            dma, dma,
            dma((tm,)), dma((tm,)),
            dma((tm,)), dma((tm,)),
            dma((seq,)), dma((seq,)),
            dma((tm,)), dma((tm,)),
        ],
        compiler_params=pltpu.CompilerParams(
            collective_id=0, has_side_effects=True, vmem_limit_bytes=64 * 1024 * 1024
        ),
    )(*arrays)
    new, adj, grad_i, grad_h, grad_b = pl.pallas_call(
        finish,
        out_shape=outs,
        in_specs=[pl.BlockSpec(memory_space=pl.ANY)] * 5,
        out_specs=(pl.BlockSpec(memory_space=pl.ANY),) * 5,
        scratch_shapes=[dma((5,))],
        compiler_params=pltpu.CompilerParams(vmem_limit_bytes=64 * 1024 * 1024),
    )(*results)
    return jnp.swapaxes(new, 1, 2), jnp.swapaxes(adj, 1, 2), grad_i, grad_h, grad_b.reshape(-1)


def solution(mesh):
    return jax.shard_map(
        functools.partial(per_device, mesh.shape["tm"], mesh.shape["seq"]),
        mesh=mesh,
        in_specs=(P("seq", "tm", None), P("seq", "tm", None), P("seq", "tm", None), P(), P(), P()),
        out_specs=(P("seq", "tm", None), P("seq", "tm", None), P(), P(), P()),
        check_vma=False,
    )
```
